128 devices in a mesh: chan: 16 (over x_hi, y, core), tm: 8 (over x_lo, z).
Axes of the slice: x: 4 (x_hi: 2, x_lo: 2; x = x_hi * 2 + x_lo), y: 4, z: 4, core: 2. Of those that a mesh axis runs over, the one named last changes fastest.
Arguments:
- record: bfloat16 [128, 4096], P('chan', 'tm'), may hold values from -6 to 6
- tail: bfloat16 [128, 255], P('chan'), may hold values from -6 to 6
- templates: bfloat16 [128, 128, 128], P(None, 'chan'), may hold values from -6 to 6
- shifts: int32 [128, 128], P(None, 'chan'), may hold values from 0 to 127
- mask: int32 [128], P('chan'), may hold values 0 or 1
Outputs:
- stack: float32 [128, 4096], P('chan', 'tm')
The draws below stay inside these ranges and needn't reach their ends.
All inputs are finite; a program needn't handle non-finite values. No bound on the sum of `mask` on one device may be relied on, other than what follows from the above.
Results may differ from the reference program's by a relative error of at most 0.0029.
Values may be sent and summed in bfloat16 or wider, within the bound.
No kernel may reach another device: no remote copies, remote signals or barrier semaphores. Data moves between devices by JAX's collectives and lax.ppermute only.
A program may use at most 64 MiB of HBM per device.

```python
import jax
import jax.numpy as jnp
from jax import lax

NCH = 128
K = 128
L = 128
MS = 128
NS = 4096
H = 255


def with_ends(entries, rng, smallest, largest):
    shape = entries.shape
    place = [jax.random.randint(jax.random.fold_in(rng, axis), (), 0, shape[axis]) for axis in range(len(shape))]
    entries = entries.at[tuple(place)].set(smallest)
    longest = shape.index(max(shape))
    place[longest] = (place[longest] + 1) % shape[longest]
    return entries.at[tuple(place)].set(largest)


def level_of(own_key, shape, cuts, least, high):
    factor_of = 1.0
    for position, parts in cuts:
        steps = jax.random.uniform(jax.random.fold_in(jax.random.fold_in(own_key, 6), position), (parts,), jnp.float32, least / len(cuts), high / len(cuts))
        factor_of = factor_of * jnp.repeat(jnp.exp(steps), shape[position] // parts).reshape((-1,) + (1,) * (len(shape) - 1 - position))
    return factor_of


def centred(stream_key, dims, scale, limit, cuts=(), kind=jnp.bfloat16):
    drawn = scale * jax.random.normal(stream_key, dims, jnp.float32)
    if cuts:
        drawn = drawn * level_of(stream_key, dims, cuts, -0.22, 0.18)
    return jnp.clip(drawn, -limit, limit).astype(kind)


def setup_inputs(seed: int = 0) -> dict:
    key_of = jax.random.split(jax.random.key(seed), 6)
    record = centred(key_of[0], (NCH, NS), 1.0, 6.0, ((0, 16), (1, 8)))
    tail = centred(key_of[1], (NCH, H), 1.0, 6.0, ((0, 16),))
    templates = centred(key_of[2], (K, NCH, L), 1.0, 6.0, ((1, 16),))
    shifts = with_ends(jax.random.randint(key_of[3], (K, NCH), 0, MS), jax.random.fold_in(key_of[3], 1), 0, MS - 1).astype(jnp.int32)
    mask = with_ends((jax.random.randint(key_of[4], (NCH,), 0, 4) < 3).astype(jnp.int32), jax.random.fold_in(key_of[4], 1), 0, 1)
    return {"record": record, "tail": tail, "templates": templates, "shifts": shifts, "mask": mask}


def unit_templates(templates):
    values = templates.astype(jnp.float32)
    tap_count = templates.shape[2]
    centered = values - lax.optimization_barrier(jnp.mean(values, axis=2, keepdims=True))
    norm = jnp.sqrt(tap_count * (lax.optimization_barrier(jnp.mean(centered * centered, axis=2, keepdims=True)) + 1e-06))
    return (centered / norm).astype(jnp.bfloat16)

def window_spread(samples, tap_count):
    values = samples.astype(jnp.float32)
    zero = jnp.zeros((1,), jnp.float32)
    sums = jnp.concatenate([zero, jnp.cumsum(values)])
    squares = jnp.concatenate([zero, jnp.cumsum(values * values)])
    window = sums[tap_count:] - sums[:-tap_count]
    power = squares[tap_count:] - squares[:-tap_count]
    return jnp.sqrt(power - window * window / tap_count + tap_count * 1e-06)

def reference(record, tail, templates, shifts, mask):
    extended = jnp.concatenate([record, tail], axis=1)
    unit = unit_templates(templates).astype(jnp.float32)
    tap_count = templates.shape[2]
    out_len = record.shape[1]
    weights = mask.astype(jnp.float32)
    total = jnp.maximum(jnp.sum(weights), 1.0)

    def pick_lags(series, start):
        return lax.dynamic_slice_in_dim(series, start, out_len)

    def add_channel(running, index):
        samples = lax.dynamic_index_in_dim(extended, index, 0, keepdims=False)
        kernel = lax.dynamic_index_in_dim(unit, index, 1, keepdims=False)
        product = lax.conv_general_dilated(samples.astype(jnp.float32)[None, None, :], kernel[:, None, :], (1,), 'VALID', preferred_element_type=jnp.float32)[0]
        spread = window_spread(samples, tap_count)
        normed = product / spread[None, :]
        offsets = lax.dynamic_index_in_dim(shifts, index, 1, keepdims=False)
        aligned = jax.vmap(pick_lags)(normed, offsets)
        weight = lax.dynamic_index_in_dim(weights, index, 0, keepdims=False)
        return (running + weight * aligned, None)
    start_acc = jnp.zeros((templates.shape[0], out_len), jnp.float32)
    running, _ = lax.scan(add_channel, start_acc, jnp.arange(record.shape[0], dtype=jnp.int32))
    return running * jnp.sqrt(tap_count / total)
```

```python
import jax
import jax.numpy as jnp
from jax import lax
from jax.experimental import pallas as pl
from jax.experimental.pallas import tpu as pltpu
from jax.sharding import PartitionSpec as P

LANES = 128
ROWS = 16


def rolled_left(x, distance):
    if distance == 0:
        return x
    return pltpu.roll(x, x.shape[1] - distance, 1)


def window_total(x, tap_count):
    width = 1
    while width < tap_count:
        x = x + rolled_left(x, width)
        width *= 2
    return x


def kernel(axis, rec_ref, nxt_ref, tail_ref, templ_ref, shift_ref, mask_ref, out_ref,
           ext_ref, unit_ref, rolled_ref, prod_ref, index_ref):
    chan_count, out_len = rec_ref.shape
    halo_len = tail_ref.shape[1]
    templ_count = out_ref.shape[0]
    tap_count = templ_ref.shape[1]
    ext_len = ext_ref.shape[1]
    lag_count = prod_ref.shape[2]
    f32 = jnp.float32

    values = templ_ref[...].astype(f32)
    centered = values - jnp.mean(values, axis=1, keepdims=True)
    power = jnp.mean(centered * centered, axis=1, keepdims=True)
    unit_ref[...] = centered * lax.rsqrt(tap_count * (power + 1e-06))

    ext_ref[:, :out_len] = rec_ref[...].astype(f32)
    at_end = lax.axis_index(axis) == lax.axis_size(axis) - 1

    @pl.when(at_end)
    def _():
        ext_ref[:, out_len:] = jnp.zeros((chan_count, ext_len - out_len), f32)
        ext_ref[:, out_len:out_len + halo_len] = tail_ref[...].astype(f32)

    @pl.when(jnp.logical_not(at_end))
    def _():
        ext_ref[:, out_len:] = nxt_ref[:, :ext_len - out_len].astype(f32)

    ext = ext_ref[...]
    weights = jnp.transpose(mask_ref[...]).astype(f32)
    window = window_total(ext, tap_count)
    squares = window_total(ext * ext, tap_count)
    scale = weights * lax.rsqrt(squares - window * window / tap_count + tap_count * 1e-06)
    for i in range(ROWS):
        shifted = rolled_left(ext, i)
        for b in range(ext_len // LANES):
            rolled_ref[b, i * chan_count:(i + 1) * chan_count, :] = shifted[:, b * LANES:(b + 1) * LANES]

    shifts = jnp.transpose(shift_ref[...])
    for c in range(chan_count):
        base = jnp.concatenate(
            [rolled_ref[b, pl.ds(c, ROWS, stride=chan_count), :] for b in range(ext_len // LANES)], axis=1)
        base = base.astype(jnp.bfloat16)
        lagged = jnp.concatenate(
            [rolled_left(base, g * ROWS)[:, :lag_count] for g in range(tap_count // ROWS)], axis=0)
        unit = unit_ref[pl.ds(c, templ_count, stride=chan_count), :].astype(jnp.bfloat16)
        product = jnp.dot(unit, lagged, preferred_element_type=f32)
        prod_ref[c] = product * scale[c:c + 1, :lag_count]
        index_ref[c] = jnp.broadcast_to(shifts[:, c:c + 1], (templ_count, LANES))

    lane = lax.broadcasted_iota(jnp.int32, (8, LANES), 1)
    blocks = out_len // LANES
    for k in range(0, templ_count, 16):
        halves = []
        for r in (k, k + 8):
            rows = slice(r, r + 8)
            totals = [jnp.zeros((8, LANES), f32)] * blocks
            for c in range(chan_count):
                shift = index_ref[c, rows, :]
                place = (lane + shift) & (LANES - 1)
                stays = lane >= shift
                for b in range(blocks):
                    here = prod_ref[c, rows, b * LANES:(b + 1) * LANES]
                    after = prod_ref[c, rows, (b + 1) * LANES:(b + 2) * LANES]
                    mixed = jnp.where(stays, here, after)
                    totals[b] = totals[b] + jnp.take_along_axis(mixed, place, axis=1)
            halves.append(jnp.concatenate(totals, axis=1))
        out_ref[k:k + 16, :out_len] = jnp.concatenate(halves, axis=0).astype(jnp.bfloat16)
    count = jnp.sum(weights, axis=0, keepdims=True)
    out_ref[:, out_len:] = jnp.broadcast_to(count, (templ_count, LANES)).astype(jnp.bfloat16)


def partial_stack(record, nxt, tail, templates, shifts, mask):
    templ_count, chan_count, tap_count = templates.shape
    out_len = record.shape[1]
    ext_len = out_len + 2 * LANES
    lag_count = out_len + LANES
    vmem = pl.BlockSpec(memory_space=pltpu.VMEM)
    return pl.pallas_call(
        lambda *refs: kernel("tm", *refs),
        out_shape=jax.ShapeDtypeStruct((templ_count, out_len + LANES), jnp.bfloat16),
        in_specs=[vmem] * 6,
        out_specs=vmem,
        scratch_shapes=[
            pltpu.VMEM((chan_count, ext_len), jnp.float32),
            pltpu.VMEM((templ_count * chan_count, tap_count), jnp.float32),
            pltpu.VMEM((ext_len // LANES, ROWS * chan_count, LANES), jnp.float32),
            pltpu.VMEM((chan_count, templ_count, lag_count), jnp.float32),
            pltpu.VMEM((chan_count, templ_count, LANES), jnp.int32),
        ],
        compiler_params=pltpu.CompilerParams(vmem_limit_bytes=32 * 1024 * 1024),
        name="partial_stack",
    )(record, nxt, tail, templates.reshape(templ_count * chan_count, tap_count), shifts.T, mask.reshape(1, -1))


def shards(record, tail, templates, shifts, mask):
    tap_count = templates.shape[2]
    out_len = record.shape[1]
    size = lax.axis_size("tm")
    nxt = lax.ppermute(record, "tm", [(i, i - 1) for i in range(1, size)])
    partial = partial_stack(record, nxt, tail, templates, shifts, mask)
    groups = lax.axis_size("chan")
    tiles = partial.reshape(groups, -1, partial.shape[1])
    arrived = lax.all_to_all(tiles, "chan", split_axis=0, concat_axis=0, tiled=True)
    summed = jnp.sum(arrived.astype(jnp.float32), axis=0)
    count = jnp.maximum(summed[:, out_len:out_len + 1], 1.0)
    return summed[:, :out_len] * jnp.sqrt(tap_count / count)


def solution(mesh):
    in_specs = (P("chan", "tm"), P("chan", None), P(None, "chan", None), P(None, "chan"), P("chan"))
    return jax.shard_map(shards, mesh=mesh, in_specs=in_specs, out_specs=P("chan", "tm"), check_vma=False)
```

```python
import jax
import jax.numpy as jnp
from jax import lax
from jax.experimental import pallas as pl
from jax.experimental.pallas import tpu as pltpu
from jax.sharding import PartitionSpec as P

LANES = 128
ROWS = 16
VMEM_BYTES = 32 * 1024 * 1024


def rolled_left(x, distance):
    if distance == 0:
        return x
    return pltpu.roll(x, x.shape[1] - distance, 1)


def window_total(x, tap_count):
    width = 1
    while width < tap_count:
        x = x + rolled_left(x, width)
        width *= 2
    return x


def window_scale(ext, weights, tap_count):
    window = window_total(ext, tap_count)
    power = window_total(ext * ext, tap_count)
    return weights * lax.rsqrt(power - window * window / tap_count + tap_count * 1e-06)


def keep_rolled(ext, rolled_ref):
    chan_count, length = ext.shape
    for i in range(ROWS):
        shifted = rolled_left(ext, i)
        for b in range(length // LANES):
            rolled_ref[b, i * chan_count:(i + 1) * chan_count, :] = shifted[:, b * LANES:(b + 1) * LANES]


def lag_matrix(rolled_ref, channel, chan_count, tap_count, lag_count):
    blocks = [rolled_ref[b, pl.ds(channel, ROWS, stride=chan_count), :] for b in range(rolled_ref.shape[0])]
    base = jnp.concatenate(blocks, axis=1).astype(jnp.bfloat16)
    pieces = [rolled_left(base, g * ROWS)[:, :lag_count] for g in range(tap_count // ROWS)]
    return jnp.concatenate(pieces, axis=0)


def aligned_sum(place, lagged_of, blocks, chan_count):
    lane = lax.broadcasted_iota(jnp.int32, (8, LANES), 1)
    totals = [jnp.zeros((8, LANES), jnp.float32)] * blocks
    for c in range(chan_count):
        shift = place(c)
        source = (lane + shift) & (LANES - 1)
        stays = lane >= shift
        for b in range(blocks):
            mixed = jnp.where(stays, lagged_of(c, b), lagged_of(c, b + 1))
            totals[b] = totals[b] + jnp.take_along_axis(mixed, source, axis=1)
    return jnp.concatenate(totals, axis=1)


def early_kernel(rec_hbm, templ_hbm, shift_hbm, mask_ref, unit_out, shift_out, border_out, first_out,
                 rec_ref, templ_ref, shift_ref, unit_ref, rolled_ref, prod_ref, sems):
    f32 = jnp.float32
    chan_count = rec_ref.shape[0]
    templ_count = first_out.shape[0]
    tap_count = templ_ref.shape[1]
    lag_count = prod_ref.shape[2]
    blocks = first_out.shape[1] // LANES
    copies = [pltpu.make_async_copy(src, dst, sems.at[n]) for n, (src, dst) in enumerate(
        ((templ_hbm, templ_ref), (rec_hbm, rec_ref), (shift_hbm, shift_ref)))]
    for copy in copies:
        copy.start()
    for copy in copies:
        copy.wait()

    values = templ_ref[...].astype(f32)
    centered = values - jnp.mean(values, axis=1, keepdims=True)
    power = jnp.mean(centered * centered, axis=1, keepdims=True)
    unit_ref[...] = centered * lax.rsqrt(tap_count * (power + 1e-06))

    ext = rec_ref[...].astype(f32)
    weights = jnp.transpose(mask_ref[...]).astype(f32)
    scale = window_scale(ext, weights, tap_count)
    keep_rolled(ext, rolled_ref)
    shifts = jnp.transpose(shift_ref[...])
    for c in range(chan_count):
        lagged = lag_matrix(rolled_ref, c, chan_count, tap_count, lag_count)
        unit = unit_ref[pl.ds(c, templ_count, stride=chan_count), :].astype(jnp.bfloat16)
        unit_out[c] = unit
        product = jnp.dot(unit, lagged, preferred_element_type=f32) * scale[c:c + 1, :lag_count]
        prod_ref[c] = product
        border_out[c] = product[:, lag_count - LANES:]
        shift_out[c] = jnp.broadcast_to(shifts[:, c:c + 1], (templ_count, LANES))
    for k in range(0, templ_count, ROWS):
        halves = [aligned_sum(lambda c: shift_out[c, r:r + 8, :],
                              lambda c, b: prod_ref[c, r:r + 8, b * LANES:(b + 1) * LANES],
                              blocks, chan_count) for r in (k, k + 8)]
        first_out[k:k + ROWS, :] = jnp.concatenate(halves, axis=0).astype(jnp.bfloat16)


def late_kernel(axis, rec_ref, nxt_ref, tail_ref, mask_ref, unit_ref, shift_ref, border_ref, first_ref, out_ref,
                ext_ref, rolled_ref, prod_ref):
    f32 = jnp.float32
    chan_count, out_len = rec_ref.shape
    halo_len = tail_ref.shape[1]
    templ_count, first_len = first_ref.shape
    tap_count = unit_ref.shape[2]
    lag_count = prod_ref.shape[2]
    blocks = lag_count // LANES
    ext_ref[:, :LANES] = rec_ref[:, out_len - LANES:].astype(f32)
    at_end = lax.axis_index(axis) == lax.axis_size(axis) - 1

    @pl.when(at_end)
    def _():
        ext_ref[:, LANES:] = jnp.zeros((chan_count, 2 * LANES), f32)
        ext_ref[:, LANES:LANES + halo_len] = tail_ref[...].astype(f32)

    @pl.when(jnp.logical_not(at_end))
    def _():
        ext_ref[:, LANES:] = nxt_ref[:, :2 * LANES].astype(f32)

    ext = ext_ref[...]
    weights = jnp.transpose(mask_ref[...]).astype(f32)
    scale = window_scale(ext, weights, tap_count)
    keep_rolled(ext, rolled_ref)
    for c in range(chan_count):
        lagged = lag_matrix(rolled_ref, c, chan_count, tap_count, lag_count)
        prod_ref[c] = jnp.dot(unit_ref[c], lagged, preferred_element_type=f32) * scale[c:c + 1, :lag_count]
    for k in range(0, templ_count, ROWS):
        def lagged_of(c, b):
            rows = slice(r, r + 8)
            return border_ref[c, rows, :] if b == 0 else prod_ref[c, rows, (b - 1) * LANES:b * LANES]
        halves = []
        for r in (k, k + 8):
            halves.append(aligned_sum(lambda c: shift_ref[c, r:r + 8, :], lagged_of, blocks, chan_count))
        out_ref[k:k + ROWS, first_len:out_len] = jnp.concatenate(halves, axis=0).astype(jnp.bfloat16)
    out_ref[:, :first_len] = first_ref[...]
    count = jnp.sum(weights, axis=0, keepdims=True)
    out_ref[:, out_len:] = jnp.broadcast_to(count, (templ_count, LANES)).astype(jnp.bfloat16)


def shards(record, tail, templates, shifts, mask):
    templ_count, chan_count, tap_count = templates.shape
    out_len = record.shape[1]
    early_len = out_len - LANES
    first_len = early_len - LANES
    f32, bf16 = jnp.float32, jnp.bfloat16
    vmem = pl.BlockSpec(memory_space=pltpu.VMEM)
    hbm = pl.BlockSpec(memory_space=pl.ANY)
    params = pltpu.CompilerParams(vmem_limit_bytes=VMEM_BYTES)
    size = lax.axis_size("tm")
    mask_row = mask.reshape(1, chan_count)
    nxt = lax.ppermute(record, "tm", [(i, i - 1) for i in range(1, size)])
    unit, moved, border, first = pl.pallas_call(
        early_kernel,
        out_shape=(
            jax.ShapeDtypeStruct((chan_count, templ_count, tap_count), bf16),
            jax.ShapeDtypeStruct((chan_count, templ_count, LANES), jnp.int32),
            jax.ShapeDtypeStruct((chan_count, templ_count, LANES), f32),
            jax.ShapeDtypeStruct((templ_count, first_len), bf16),
        ),
        in_specs=[hbm] * 3 + [vmem],
        out_specs=(vmem,) * 4,
        scratch_shapes=[
            pltpu.VMEM((chan_count, out_len), bf16),
            pltpu.VMEM((templ_count * chan_count, tap_count), bf16),
            pltpu.VMEM((chan_count, templ_count), jnp.int32),
            pltpu.VMEM((templ_count * chan_count, tap_count), f32),
            pltpu.VMEM((out_len // LANES, ROWS * chan_count, LANES), f32),
            pltpu.VMEM((chan_count, templ_count, early_len), f32),
            pltpu.SemaphoreType.DMA((3,)),
        ],
        compiler_params=params,
        cost_estimate=pl.CostEstimate(flops=200_000_000, bytes_accessed=2_000_000, transcendentals=0),
        name="early_lags",
    )(record, templates.reshape(templ_count * chan_count, tap_count), shifts.T, mask_row)
    partial = pl.pallas_call(
        lambda *refs: late_kernel("tm", *refs),
        out_shape=jax.ShapeDtypeStruct((templ_count, out_len + LANES), bf16),
        in_specs=[vmem] * 8,
        out_specs=vmem,
        scratch_shapes=[
            pltpu.VMEM((chan_count, 3 * LANES), f32),
            pltpu.VMEM((3, ROWS * chan_count, LANES), f32),
            pltpu.VMEM((chan_count, templ_count, 2 * LANES), f32),
        ],
        compiler_params=params,
        name="late_lags",
    )(record, nxt, tail, mask_row, unit, moved, border, first)
    tiles = partial.reshape(lax.axis_size("chan"), -1, partial.shape[1])
    arrived = lax.all_to_all(tiles, "chan", split_axis=0, concat_axis=0, tiled=True)
    summed = jnp.sum(arrived.astype(f32), axis=0)
    count = jnp.maximum(summed[:, out_len:out_len + 1], 1.0)
    return summed[:, :out_len] * jnp.sqrt(tap_count / count)


def solution(mesh):
    in_specs = (P("chan", "tm"), P("chan", None), P(None, "chan", None), P(None, "chan"), P("chan"))
    return jax.shard_map(shards, mesh=mesh, in_specs=in_specs, out_specs=P("chan", "tm"), check_vma=False)
```

```python
import jax
import jax.numpy as jnp
from jax import lax
from jax.experimental import pallas as pl
from jax.experimental.pallas import tpu as pltpu
from jax.sharding import PartitionSpec as P

LANES = 128
ROWS = 16
VMEM_BYTES = 32 * 1024 * 1024


def rolled_left(x, distance):
    if distance == 0:
        return x
    return pltpu.roll(x, x.shape[1] - distance, 1)


def window_total(x, tap_count):
    width = 1
    while width < tap_count:
        x = x + rolled_left(x, width)
        width *= 2
    return x


def window_scale(ext, weights, tap_count):
    window = window_total(ext, tap_count)
    power = window_total(ext * ext, tap_count)
    return weights * lax.rsqrt(power - window * window / tap_count + tap_count * 1e-06)


def keep_rolled(ext, rolled_ref):
    chan_count, length = ext.shape
    for i in range(ROWS):
        shifted = rolled_left(ext, i)
        for b in range(length // LANES):
            rolled_ref[b, i * chan_count:(i + 1) * chan_count, :] = shifted[:, b * LANES:(b + 1) * LANES]


def lag_matrix(rolled_ref, channel, chan_count, tap_count, lag_count):
    blocks = [rolled_ref[b, pl.ds(channel, ROWS, stride=chan_count), :] for b in range(rolled_ref.shape[0])]
    base = jnp.concatenate(blocks, axis=1).astype(jnp.bfloat16)
    pieces = [rolled_left(base, g * ROWS)[:, :lag_count] for g in range(tap_count // ROWS)]
    return jnp.concatenate(pieces, axis=0)


def aligned_sum(place, lagged_of, blocks, chan_count):
    lane = lax.broadcasted_iota(jnp.int32, (8, LANES), 1)
    totals = [jnp.zeros((8, LANES), jnp.float32)] * blocks
    for c in range(chan_count):
        shift = place(c)
        source = (lane + shift) & (LANES - 1)
        stays = lane >= shift
        for b in range(blocks):
            mixed = jnp.where(stays, lagged_of(c, b), lagged_of(c, b + 1))
            totals[b] = totals[b] + jnp.take_along_axis(mixed, source, axis=1)
    return jnp.concatenate(totals, axis=1)


def early_kernel(rec_hbm, tail_hbm, templ_hbm, shift_hbm, mask_hbm,
                 unit_out, shift_out, border_out, first_out, edge_out, weight_out,
                 rec_ref, tail_ref, templ_ref, shift_ref, mask_ref, unit_ref, rolled_ref, prod_ref, sems):
    f32 = jnp.float32
    chan_count = rec_ref.shape[0]
    templ_count = first_out.shape[0]
    tap_count = templ_ref.shape[1]
    lag_count = prod_ref.shape[2]
    blocks = first_out.shape[1] // LANES
    copies = [pltpu.make_async_copy(src, dst, sems.at[n]) for n, (src, dst) in enumerate(
        ((templ_hbm, templ_ref), (rec_hbm, rec_ref), (shift_hbm, shift_ref), (mask_hbm, mask_ref), (tail_hbm, tail_ref)))]
    for copy in copies:
        copy.start()
    for copy in copies:
        copy.wait()

    values = templ_ref[...].astype(f32)
    centered = values - jnp.mean(values, axis=1, keepdims=True)
    power = jnp.mean(centered * centered, axis=1, keepdims=True)
    unit_ref[...] = centered * lax.rsqrt(tap_count * (power + 1e-06))

    ext = rec_ref[...].astype(f32)
    weights = jnp.transpose(mask_ref[...]).astype(f32)
    weight_out[...] = jnp.broadcast_to(weights, (chan_count, LANES))
    halo_len = tail_ref.shape[1]
    edge_out[...] = jnp.zeros(edge_out.shape, f32)
    edge_out[:, :LANES] = ext[:, ext.shape[1] - LANES:]
    edge_out[:, LANES:LANES + halo_len] = tail_ref[...].astype(f32)
    scale = window_scale(ext, weights, tap_count)
    keep_rolled(ext, rolled_ref)
    shifts = jnp.transpose(shift_ref[...])
    for c in range(chan_count):
        lagged = lag_matrix(rolled_ref, c, chan_count, tap_count, lag_count)
        unit = unit_ref[pl.ds(c, templ_count, stride=chan_count), :].astype(jnp.bfloat16)
        unit_out[c] = unit
        product = jnp.dot(unit, lagged, preferred_element_type=f32) * scale[c:c + 1, :lag_count]
        prod_ref[c] = product
        border_out[c] = product[:, lag_count - LANES:]
        shift_out[c] = jnp.broadcast_to(shifts[:, c:c + 1], (templ_count, LANES))
    for k in range(0, templ_count, ROWS):
        halves = [aligned_sum(lambda c: shift_out[c, r:r + 8, :],
                              lambda c, b: prod_ref[c, r:r + 8, b * LANES:(b + 1) * LANES],
                              blocks, chan_count) for r in (k, k + 8)]
        first_out[k:k + ROWS, :] = jnp.concatenate(halves, axis=0).astype(jnp.bfloat16)


def late_kernel(axis, nxt_ref, edge_ref, weight_ref, unit_ref, shift_ref, border_ref, first_ref, out_ref,
                ext_ref, rolled_ref, prod_ref):
    f32 = jnp.float32
    chan_count = nxt_ref.shape[0]
    templ_count, first_len = first_ref.shape
    tap_count = unit_ref.shape[2]
    lag_count = prod_ref.shape[2]
    blocks = lag_count // LANES
    out_len = first_len + lag_count
    at_end = lax.axis_index(axis) == lax.axis_size(axis) - 1
    ext_ref[...] = edge_ref[...]

    @pl.when(jnp.logical_not(at_end))
    def _():
        ext_ref[:, LANES:] = nxt_ref[:, :2 * LANES].astype(f32)

    ext = ext_ref[...]
    weights = weight_ref[...]
    scale = window_scale(ext, weights[:, :1], tap_count)
    keep_rolled(ext, rolled_ref)
    for c in range(chan_count):
        lagged = lag_matrix(rolled_ref, c, chan_count, tap_count, lag_count)
        prod_ref[c] = jnp.dot(unit_ref[c], lagged, preferred_element_type=f32) * scale[c:c + 1, :lag_count]
    for k in range(0, templ_count, ROWS):
        def lagged_of(c, b):
            rows = slice(r, r + 8)
            return border_ref[c, rows, :] if b == 0 else prod_ref[c, rows, (b - 1) * LANES:b * LANES]
        halves = []
        for r in (k, k + 8):
            halves.append(aligned_sum(lambda c: shift_ref[c, r:r + 8, :], lagged_of, blocks, chan_count))
        out_ref[k:k + ROWS, first_len:out_len] = jnp.concatenate(halves, axis=0).astype(jnp.bfloat16)
    out_ref[:, :first_len] = first_ref[...]
    count = jnp.sum(weights, axis=0, keepdims=True)
    out_ref[:, out_len:] = jnp.broadcast_to(count, (templ_count, LANES)).astype(jnp.bfloat16)


def shards(record, tail, templates, shifts, mask):
    templ_count, chan_count, tap_count = templates.shape
    out_len = record.shape[1]
    early_len = out_len - LANES
    first_len = early_len - LANES
    f32, bf16 = jnp.float32, jnp.bfloat16
    vmem = pl.BlockSpec(memory_space=pltpu.VMEM)
    hbm = pl.BlockSpec(memory_space=pltpu.HBM)
    params = pltpu.CompilerParams(vmem_limit_bytes=VMEM_BYTES)
    size = lax.axis_size("tm")
    mask_row = mask.reshape(1, chan_count)
    nxt = lax.ppermute(record, "tm", [(i, i - 1) for i in range(1, size)])
    unit, moved, border, first, edge, weights = pl.pallas_call(
        early_kernel,
        out_shape=(
            jax.ShapeDtypeStruct((chan_count, templ_count, tap_count), bf16),
            jax.ShapeDtypeStruct((chan_count, templ_count, LANES), jnp.int32),
            jax.ShapeDtypeStruct((chan_count, templ_count, LANES), f32),
            jax.ShapeDtypeStruct((templ_count, first_len), bf16),
            jax.ShapeDtypeStruct((chan_count, 3 * LANES), f32),
            jax.ShapeDtypeStruct((chan_count, LANES), f32),
        ),
        in_specs=[hbm] * 5,
        out_specs=(vmem,) * 6,
        scratch_shapes=[
            pltpu.VMEM((chan_count, out_len), bf16),
            pltpu.VMEM(tail.shape, bf16),
            pltpu.VMEM((templ_count * chan_count, tap_count), bf16),
            pltpu.VMEM((chan_count, templ_count), jnp.int32),
            pltpu.VMEM((1, chan_count), jnp.int32),
            pltpu.VMEM((templ_count * chan_count, tap_count), f32),
            pltpu.VMEM((out_len // LANES, ROWS * chan_count, LANES), f32),
            pltpu.VMEM((chan_count, templ_count, early_len), f32),
            pltpu.SemaphoreType.DMA((5,)),
        ],
        compiler_params=params,
        cost_estimate=pl.CostEstimate(flops=200_000_000, bytes_accessed=2_000_000, transcendentals=0),
        name="early_lags",
    )(*[pltpu.with_memory_space_constraint(x, pltpu.HBM) for x in (
        record, tail, templates.reshape(templ_count * chan_count, tap_count), shifts.T, mask_row)])
    partial = pl.pallas_call(
        lambda *refs: late_kernel("tm", *refs),
        out_shape=jax.ShapeDtypeStruct((templ_count, out_len + LANES), bf16),
        in_specs=[vmem] * 7,
        out_specs=vmem,
        scratch_shapes=[
            pltpu.VMEM((chan_count, 3 * LANES), f32),
            pltpu.VMEM((3, ROWS * chan_count, LANES), f32),
            pltpu.VMEM((chan_count, templ_count, 2 * LANES), f32),
        ],
        compiler_params=params,
        name="late_lags",
    )(nxt, edge, weights, unit, moved, border, first)
    tiles = partial.reshape(lax.axis_size("chan"), -1, partial.shape[1])
    arrived = lax.all_to_all(tiles, "chan", split_axis=0, concat_axis=0, tiled=True)
    summed = jnp.sum(arrived.astype(f32), axis=0)
    count = jnp.maximum(summed[:, out_len:out_len + 1], 1.0)
    return summed[:, :out_len] * jnp.sqrt(tap_count / count)


def solution(mesh):
    in_specs = (P("chan", "tm"), P("chan", None), P(None, "chan", None), P(None, "chan"), P("chan"))
    return jax.shard_map(shards, mesh=mesh, in_specs=in_specs, out_specs=P("chan", "tm"), check_vma=False)
```

```python
import jax
import jax.numpy as jnp
from jax import lax
from jax.experimental import pallas as pl
from jax.experimental.pallas import tpu as pltpu
from jax.sharding import PartitionSpec as P

LANES = 128
ROWS = 16
VMEM_BYTES = 32 * 1024 * 1024


def rolled_left(x, distance):
    if distance == 0:
        return x
    return pltpu.roll(x, x.shape[1] - distance, 1)


def window_total(x, tap_count):
    width = 1
    while width < tap_count:
        x = x + rolled_left(x, width)
        width *= 2
    return x


def window_scale(ext, weights, tap_count):
    window = window_total(ext, tap_count)
    power = window_total(ext * ext, tap_count)
    return weights * lax.rsqrt(power - window * window / tap_count + tap_count * 1e-06)


def keep_rolled(ext, rolled_ref):
    chan_count, length = ext.shape
    for i in range(ROWS):
        shifted = rolled_left(ext, i)
        for b in range(length // LANES):
            rolled_ref[b, i * chan_count:(i + 1) * chan_count, :] = shifted[:, b * LANES:(b + 1) * LANES]


def lag_matrix(rolled_ref, channel, chan_count, tap_count, lag_count):
    blocks = [rolled_ref[b, pl.ds(channel, ROWS, stride=chan_count), :] for b in range(rolled_ref.shape[0])]
    base = jnp.concatenate(blocks, axis=1).astype(jnp.bfloat16)
    pieces = [rolled_left(base, g * ROWS)[:, :lag_count] for g in range(tap_count // ROWS)]
    return jnp.concatenate(pieces, axis=0)


def aligned_sum(place, lagged_of, blocks, chan_count):
    lane = lax.broadcasted_iota(jnp.int32, (8, LANES), 1)
    totals = [jnp.zeros((8, LANES), jnp.float32)] * blocks
    for c in range(chan_count):
        shift = place(c)
        source = (lane + shift) & (LANES - 1)
        stays = lane >= shift
        for b in range(blocks):
            mixed = jnp.where(stays, lagged_of(c, b), lagged_of(c, b + 1))
            totals[b] = totals[b] + jnp.take_along_axis(mixed, source, axis=1, mode="promise_in_bounds")
    return jnp.concatenate(totals, axis=1)


def early_kernel(rec_hbm, tail_hbm, templ_hbm, shift_hbm, mask_hbm,
                 unit_out, shift_out, border_out, first_out, edge_out, weight_out,
                 rec_ref, tail_ref, templ_ref, shift_ref, mask_ref, unit_ref, rolled_ref, prod_ref, sems):
    f32 = jnp.float32
    chan_count = rec_ref.shape[0]
    templ_count = first_out.shape[0]
    tap_count = templ_ref.shape[1]
    lag_count = prod_ref.shape[2]
    blocks = first_out.shape[1] // LANES
    copies = [pltpu.make_async_copy(src, dst, sems.at[n]) for n, (src, dst) in enumerate(
        ((templ_hbm, templ_ref), (rec_hbm, rec_ref), (shift_hbm, shift_ref), (mask_hbm, mask_ref), (tail_hbm, tail_ref)))]
    for copy in copies:
        copy.start()
    for copy in copies:
        copy.wait()

    values = templ_ref[...].astype(f32)
    ones = jnp.ones((tap_count, LANES), jnp.bfloat16)
    centered = values - jnp.dot(templ_ref[...], ones, preferred_element_type=f32) / tap_count
    squares = centered * centered
    high = squares.astype(jnp.bfloat16)
    low = (squares - high.astype(f32)).astype(jnp.bfloat16)
    power = (jnp.dot(high, ones, preferred_element_type=f32) + jnp.dot(low, ones, preferred_element_type=f32)) / tap_count
    unit_ref[...] = centered * lax.rsqrt(tap_count * (power + 1e-06))

    ext = rec_ref[...].astype(f32)
    weights = jnp.transpose(mask_ref[...]).astype(f32)
    weight_out[...] = jnp.broadcast_to(weights, (chan_count, LANES))
    halo_len = tail_ref.shape[1]
    edge_out[...] = jnp.zeros(edge_out.shape, f32)
    edge_out[:, :LANES] = ext[:, ext.shape[1] - LANES:]
    edge_out[:, LANES:LANES + halo_len] = tail_ref[...].astype(f32)
    scale = window_scale(ext, weights, tap_count)
    keep_rolled(ext, rolled_ref)
    shifts = jnp.transpose(shift_ref[...]).astype(f32).astype(jnp.bfloat16)
    pick = lax.broadcasted_iota(jnp.int32, (chan_count, chan_count * LANES), 1) // LANES
    pick = (pick == lax.broadcasted_iota(jnp.int32, pick.shape, 0)).astype(f32).astype(jnp.bfloat16)
    spread_shifts = jnp.dot(shifts, pick, preferred_element_type=f32).astype(jnp.int32)
    for c in range(chan_count):
        lagged = lag_matrix(rolled_ref, c, chan_count, tap_count, lag_count)
        unit = unit_ref[pl.ds(c, templ_count, stride=chan_count), :].astype(jnp.bfloat16)
        unit_out[c] = unit
        product = jnp.dot(unit, lagged, preferred_element_type=f32) * scale[c:c + 1, :lag_count]
        prod_ref[c] = product
        border_out[c] = product[:, lag_count - LANES:]
        shift_out[c] = spread_shifts[:, c * LANES:(c + 1) * LANES]
    for k in range(0, templ_count, ROWS):
        halves = [aligned_sum(lambda c: shift_out[c, r:r + 8, :],
                              lambda c, b: prod_ref[c, r:r + 8, b * LANES:(b + 1) * LANES],
                              blocks, chan_count) for r in (k, k + 8)]
        first_out[k:k + ROWS, :] = jnp.concatenate(halves, axis=0).astype(jnp.bfloat16)


def late_kernel(axis, nxt_ref, edge_ref, weight_ref, unit_ref, shift_ref, border_ref, first_ref, out_ref,
                ext_ref, rolled_ref, prod_ref):
    f32 = jnp.float32
    chan_count = nxt_ref.shape[0]
    templ_count, first_len = first_ref.shape
    tap_count = unit_ref.shape[2]
    lag_count = prod_ref.shape[2]
    blocks = lag_count // LANES
    out_len = first_len + lag_count
    at_end = lax.axis_index(axis) == lax.axis_size(axis) - 1
    ext_ref[...] = edge_ref[...]

    @pl.when(jnp.logical_not(at_end))
    def _():
        ext_ref[:, LANES:] = nxt_ref[:, :2 * LANES].astype(f32)

    ext = ext_ref[...]
    weights = weight_ref[...]
    scale = window_scale(ext, weights[:, :1], tap_count)
    keep_rolled(ext, rolled_ref)
    for c in range(chan_count):
        lagged = lag_matrix(rolled_ref, c, chan_count, tap_count, lag_count)
        prod_ref[c] = jnp.dot(unit_ref[c], lagged, preferred_element_type=f32) * scale[c:c + 1, :lag_count]
    for k in range(0, templ_count, ROWS):
        def lagged_of(c, b):
            rows = slice(r, r + 8)
            return border_ref[c, rows, :] if b == 0 else prod_ref[c, rows, (b - 1) * LANES:b * LANES]
        halves = []
        for r in (k, k + 8):
            halves.append(aligned_sum(lambda c: shift_ref[c, r:r + 8, :], lagged_of, blocks, chan_count))
        out_ref[k:k + ROWS, first_len:out_len] = jnp.concatenate(halves, axis=0).astype(jnp.bfloat16)
    out_ref[:, :first_len] = first_ref[...]
    count = jnp.sum(weights, axis=0, keepdims=True)
    out_ref[:, out_len:] = jnp.broadcast_to(count, (templ_count, LANES)).astype(jnp.bfloat16)


def shards(record, tail, templates, shifts, mask):
    templ_count, chan_count, tap_count = templates.shape
    out_len = record.shape[1]
    early_len = out_len - LANES
    first_len = early_len - LANES
    f32, bf16 = jnp.float32, jnp.bfloat16
    vmem = pl.BlockSpec(memory_space=pltpu.VMEM)
    hbm = pl.BlockSpec(memory_space=pltpu.HBM)
    params = pltpu.CompilerParams(vmem_limit_bytes=VMEM_BYTES)
    size = lax.axis_size("tm")
    mask_row = mask.reshape(1, chan_count)
    nxt = lax.ppermute(record, "tm", [(i, i - 1) for i in range(1, size)])
    unit, moved, border, first, edge, weights = pl.pallas_call(
        early_kernel,
        out_shape=(
            jax.ShapeDtypeStruct((chan_count, templ_count, tap_count), bf16),
            jax.ShapeDtypeStruct((chan_count, templ_count, LANES), jnp.int32),
            jax.ShapeDtypeStruct((chan_count, templ_count, LANES), f32),
            jax.ShapeDtypeStruct((templ_count, first_len), bf16),
            jax.ShapeDtypeStruct((chan_count, 3 * LANES), f32),
            jax.ShapeDtypeStruct((chan_count, LANES), f32),
        ),
        in_specs=[hbm] * 5,
        out_specs=(vmem,) * 6,
        scratch_shapes=[
            pltpu.VMEM((chan_count, out_len), bf16),
            pltpu.VMEM(tail.shape, bf16),
            pltpu.VMEM((templ_count * chan_count, tap_count), bf16),
            pltpu.VMEM((chan_count, templ_count), jnp.int32),
            pltpu.VMEM((1, chan_count), jnp.int32),
            pltpu.VMEM((templ_count * chan_count, tap_count), f32),
            pltpu.VMEM((out_len // LANES, ROWS * chan_count, LANES), f32),
            pltpu.VMEM((chan_count, templ_count, early_len), f32),
            pltpu.SemaphoreType.DMA((5,)),
        ],
        compiler_params=params,
        cost_estimate=pl.CostEstimate(flops=200_000_000, bytes_accessed=2_000_000, transcendentals=0),
        name="early_lags",
    )(*[pltpu.with_memory_space_constraint(x, pltpu.HBM) for x in (
        record, tail, templates.reshape(templ_count * chan_count, tap_count), shifts.T, mask_row)])
    partial = pl.pallas_call(
        lambda *refs: late_kernel("tm", *refs),
        out_shape=jax.ShapeDtypeStruct((templ_count, out_len + LANES), bf16),
        in_specs=[vmem] * 7,
        out_specs=vmem,
        scratch_shapes=[
            pltpu.VMEM((chan_count, 3 * LANES), f32),
            pltpu.VMEM((3, ROWS * chan_count, LANES), f32),
            pltpu.VMEM((chan_count, templ_count, 2 * LANES), f32),
        ],
        compiler_params=params,
        name="late_lags",
    )(nxt, edge, weights, unit, moved, border, first)
    tiles = partial.reshape(lax.axis_size("chan"), -1, partial.shape[1])
    arrived = lax.all_to_all(tiles, "chan", split_axis=0, concat_axis=0, tiled=True)
    summed = jnp.sum(arrived.astype(f32), axis=0)
    count = jnp.maximum(summed[:, out_len:out_len + 1], 1.0)
    return summed[:, :out_len] * jnp.sqrt(tap_count / count)


def solution(mesh):
    in_specs = (P("chan", "tm"), P("chan", None), P(None, "chan", None), P(None, "chan"), P("chan"))
    return jax.shard_map(shards, mesh=mesh, in_specs=in_specs, out_specs=P("chan", "tm"), check_vma=False)
```

```python
import jax
import jax.numpy as jnp
from jax import lax
from jax.experimental import pallas as pl
from jax.experimental.pallas import tpu as pltpu
from jax.sharding import PartitionSpec as P

LANES = 128
ROWS = 16
VMEM_BYTES = 32 * 1024 * 1024


def rolled_left(x, distance):
    if distance == 0:
        return x
    return pltpu.roll(x, x.shape[1] - distance, 1)


def window_total(x, tap_count):
    width = 1
    while width < tap_count:
        x = x + rolled_left(x, width)
        width *= 2
    return x


def window_scale(ext, weights, tap_count):
    window = window_total(ext, tap_count)
    power = window_total(ext * ext, tap_count)
    return weights * lax.rsqrt(power - window * window / tap_count + tap_count * 1e-06)


def keep_rolled(ext, rolled_ref):
    chan_count, length = ext.shape
    for i in range(ROWS):
        shifted = rolled_left(ext, i)
        for b in range(length // LANES):
            rolled_ref[b, i * chan_count:(i + 1) * chan_count, :] = shifted[:, b * LANES:(b + 1) * LANES]


def lag_matrix(rolled_ref, channel, chan_count, tap_count, lag_count):
    blocks = [rolled_ref[b, pl.ds(channel, ROWS, stride=chan_count), :] for b in range(rolled_ref.shape[0])]
    base = jnp.concatenate(blocks, axis=1).astype(jnp.bfloat16)
    pieces = [rolled_left(base, g * ROWS)[:, :lag_count] for g in range(tap_count // ROWS)]
    return jnp.concatenate(pieces, axis=0)


def aligned_sum(place, lagged_of, blocks, chan_count):
    lane = lax.broadcasted_iota(jnp.int32, (8, LANES), 1)
    totals = [jnp.zeros((8, LANES), jnp.float32)] * blocks
    for c in range(chan_count):
        shift = place(c)
        source = (lane + shift) & (LANES - 1)
        stays = lane >= shift
        for b in range(blocks):
            mixed = jnp.where(stays, lagged_of(c, b), lagged_of(c, b + 1))
            totals[b] = totals[b] + jnp.take_along_axis(mixed, source, axis=1, mode="promise_in_bounds")
    return jnp.concatenate(totals, axis=1)


def early_kernel(rec_hbm, tail_hbm, templ_hbm, shift_hbm, mask_hbm,
                 unit_out, shift_out, border_out, first_out, edge_out, weight_out, band_out,
                 rec_ref, tail_ref, templ_ref, shift_ref, mask_ref, unit_ref, rolled_ref, prod_ref, sems):
    f32 = jnp.float32
    chan_count = rec_ref.shape[0]
    templ_count = first_out.shape[0]
    tap_count = templ_ref.shape[1]
    lag_count = prod_ref.shape[2]
    blocks = first_out.shape[1] // LANES
    copies = [pltpu.make_async_copy(src, dst, sems.at[n]) for n, (src, dst) in enumerate(
        ((templ_hbm, templ_ref), (rec_hbm, rec_ref), (shift_hbm, shift_ref), (mask_hbm, mask_ref), (tail_hbm, tail_ref)))]
    for copy in copies:
        copy.start()
    for copy in copies:
        copy.wait()

    values = templ_ref[...].astype(f32)
    ones = jnp.ones((tap_count, LANES), jnp.bfloat16)
    centered = values - jnp.dot(templ_ref[...], ones, preferred_element_type=f32) / tap_count
    squares = centered * centered
    high = squares.astype(jnp.bfloat16)
    low = (squares - high.astype(f32)).astype(jnp.bfloat16)
    power = (jnp.dot(high, ones, preferred_element_type=f32) + jnp.dot(low, ones, preferred_element_type=f32)) / tap_count
    unit_ref[...] = centered * lax.rsqrt(tap_count * (power + 1e-06))

    ext = rec_ref[...].astype(f32)
    weights = jnp.transpose(mask_ref[...]).astype(f32)
    span = lax.broadcasted_iota(jnp.int32, band_out.shape, 0) - lax.broadcasted_iota(jnp.int32, band_out.shape, 1)
    band_out[...] = jnp.where((span >= 0) & (span < tap_count), 1.0, 0.0).astype(jnp.bfloat16)
    weight_out[...] = jnp.broadcast_to(weights, (chan_count, LANES))
    halo_len = tail_ref.shape[1]
    edge_out[...] = jnp.zeros(edge_out.shape, f32)
    edge_out[:, :LANES] = ext[:, ext.shape[1] - LANES:]
    edge_out[:, LANES:LANES + halo_len] = tail_ref[...].astype(f32)
    scale = window_scale(ext, weights, tap_count)
    keep_rolled(ext, rolled_ref)
    shifts = jnp.transpose(shift_ref[...]).astype(f32).astype(jnp.bfloat16)
    pick = lax.broadcasted_iota(jnp.int32, (chan_count, chan_count * LANES), 1) // LANES
    pick = (pick == lax.broadcasted_iota(jnp.int32, pick.shape, 0)).astype(f32).astype(jnp.bfloat16)
    spread_shifts = jnp.dot(shifts, pick, preferred_element_type=f32).astype(jnp.int32)
    for c in range(chan_count):
        lagged = lag_matrix(rolled_ref, c, chan_count, tap_count, lag_count)
        unit = unit_ref[pl.ds(c, templ_count, stride=chan_count), :].astype(jnp.bfloat16)
        unit_out[c] = unit
        product = jnp.dot(unit, lagged, preferred_element_type=f32) * scale[c:c + 1, :lag_count]
        prod_ref[c] = product
        border_out[c] = product[:, lag_count - LANES:]
        shift_out[c] = spread_shifts[:, c * LANES:(c + 1) * LANES]
    for k in range(0, templ_count, ROWS):
        halves = [aligned_sum(lambda c: shift_out[c, r:r + 8, :],
                              lambda c, b: prod_ref[c, r:r + 8, b * LANES:(b + 1) * LANES],
                              blocks, chan_count) for r in (k, k + 8)]
        first_out[k:k + ROWS, :] = jnp.concatenate(halves, axis=0).astype(jnp.bfloat16)


def late_kernel(axis, nxt_ref, edge_ref, weight_ref, unit_ref, shift_ref, border_ref, first_ref, band_ref, out_ref,
                ext_ref, rolled_ref, prod_ref):
    f32 = jnp.float32
    chan_count = nxt_ref.shape[0]
    templ_count, first_len = first_ref.shape
    tap_count = unit_ref.shape[2]
    lag_count = prod_ref.shape[2]
    blocks = lag_count // LANES
    out_len = first_len + lag_count
    at_end = lax.axis_index(axis) == lax.axis_size(axis) - 1
    ext_ref[...] = edge_ref[...]

    @pl.when(jnp.logical_not(at_end))
    def _():
        ext_ref[:, LANES:] = nxt_ref[:, :2 * LANES].astype(f32)

    ext = ext_ref[...]
    weights = weight_ref[...]
    squares = ext * ext
    high = squares.astype(jnp.bfloat16).astype(f32)
    stacked = jnp.concatenate([ext, high, squares - high, jnp.zeros_like(ext)], axis=0).astype(jnp.bfloat16)
    totals = jnp.dot(stacked, band_ref[...], preferred_element_type=f32)
    window = totals[:chan_count]
    power = totals[chan_count:2 * chan_count] + totals[2 * chan_count:3 * chan_count]
    scale = weights[:, :1] * lax.rsqrt(power - window * window / tap_count + tap_count * 1e-06)
    keep_rolled(ext, rolled_ref)
    for c in range(chan_count):
        lagged = lag_matrix(rolled_ref, c, chan_count, tap_count, lag_count)
        prod_ref[c] = jnp.dot(unit_ref[c], lagged, preferred_element_type=f32) * scale[c:c + 1, :lag_count]
    for k in range(0, templ_count, ROWS):
        def lagged_of(c, b):
            rows = slice(r, r + 8)
            return border_ref[c, rows, :] if b == 0 else prod_ref[c, rows, (b - 1) * LANES:b * LANES]
        halves = []
        for r in (k, k + 8):
            halves.append(aligned_sum(lambda c: shift_ref[c, r:r + 8, :], lagged_of, blocks, chan_count))
        out_ref[k:k + ROWS, first_len:out_len] = jnp.concatenate(halves, axis=0).astype(jnp.bfloat16)
    out_ref[:, :first_len] = first_ref[...]
    count = jnp.sum(weights, axis=0, keepdims=True)
    out_ref[:, out_len:] = jnp.broadcast_to(count, (templ_count, LANES)).astype(jnp.bfloat16)


def shards(record, tail, templates, shifts, mask):
    templ_count, chan_count, tap_count = templates.shape
    out_len = record.shape[1]
    early_len = out_len - LANES
    first_len = early_len - LANES
    f32, bf16 = jnp.float32, jnp.bfloat16
    vmem = pl.BlockSpec(memory_space=pltpu.VMEM)
    hbm = pl.BlockSpec(memory_space=pltpu.HBM)
    params = pltpu.CompilerParams(vmem_limit_bytes=VMEM_BYTES)
    size = lax.axis_size("tm")
    mask_row = mask.reshape(1, chan_count)
    nxt = lax.ppermute(record, "tm", [(i, i - 1) for i in range(1, size)])
    unit, moved, border, first, edge, weights, band = pl.pallas_call(
        early_kernel,
        out_shape=(
            jax.ShapeDtypeStruct((chan_count, templ_count, tap_count), bf16),
            jax.ShapeDtypeStruct((chan_count, templ_count, LANES), jnp.int32),
            jax.ShapeDtypeStruct((chan_count, templ_count, LANES), f32),
            jax.ShapeDtypeStruct((templ_count, first_len), bf16),
            jax.ShapeDtypeStruct((chan_count, 3 * LANES), f32),
            jax.ShapeDtypeStruct((chan_count, LANES), f32),
            jax.ShapeDtypeStruct((3 * LANES, 2 * LANES), bf16),
        ),
        in_specs=[hbm] * 5,
        out_specs=(vmem,) * 7,
        scratch_shapes=[
            pltpu.VMEM((chan_count, out_len), bf16),
            pltpu.VMEM(tail.shape, bf16),
            pltpu.VMEM((templ_count * chan_count, tap_count), bf16),
            pltpu.VMEM((chan_count, templ_count), jnp.int32),
            pltpu.VMEM((1, chan_count), jnp.int32),
            pltpu.VMEM((templ_count * chan_count, tap_count), f32),
            pltpu.VMEM((out_len // LANES, ROWS * chan_count, LANES), f32),
            pltpu.VMEM((chan_count, templ_count, early_len), f32),
            pltpu.SemaphoreType.DMA((5,)),
        ],
        compiler_params=params,
        cost_estimate=pl.CostEstimate(flops=200_000_000, bytes_accessed=2_000_000, transcendentals=0),
        name="early_lags",
    )(*[pltpu.with_memory_space_constraint(x, pltpu.HBM) for x in (
        record, tail, templates.reshape(templ_count * chan_count, tap_count), shifts.T, mask_row)])
    partial = pl.pallas_call(
        lambda *refs: late_kernel("tm", *refs),
        out_shape=jax.ShapeDtypeStruct((templ_count, out_len + LANES), bf16),
        in_specs=[vmem] * 8,
        out_specs=vmem,
        scratch_shapes=[
            pltpu.VMEM((chan_count, 3 * LANES), f32),
            pltpu.VMEM((3, ROWS * chan_count, LANES), f32),
            pltpu.VMEM((chan_count, templ_count, 2 * LANES), f32),
        ],
        compiler_params=params,
        name="late_lags",
    )(nxt, edge, weights, unit, moved, border, first, band)
    tiles = partial.reshape(lax.axis_size("chan"), -1, partial.shape[1])
    arrived = lax.all_to_all(tiles, "chan", split_axis=0, concat_axis=0, tiled=True)
    summed = jnp.sum(arrived.astype(f32), axis=0)
    count = jnp.maximum(summed[:, out_len:out_len + 1], 1.0)
    return summed[:, :out_len] * jnp.sqrt(tap_count / count)


def solution(mesh):
    in_specs = (P("chan", "tm"), P("chan", None), P(None, "chan", None), P(None, "chan"), P("chan"))
    return jax.shard_map(shards, mesh=mesh, in_specs=in_specs, out_specs=P("chan", "tm"), check_vma=False)
```

```python
import jax
import jax.numpy as jnp
from jax import lax
from jax.experimental import pallas as pl
from jax.experimental.pallas import tpu as pltpu
from jax.sharding import PartitionSpec as P

LANES = 128
ROWS = 16
VMEM_BYTES = 32 * 1024 * 1024


def rolled_left(x, distance):
    if distance == 0:
        return x
    return pltpu.roll(x, x.shape[1] - distance, 1)


def window_total(x, tap_count):
    width = 1
    while width < tap_count:
        x = x + rolled_left(x, width)
        width *= 2
    return x


def window_scale(ext, weights, tap_count):
    window = window_total(ext, tap_count)
    power = window_total(ext * ext, tap_count)
    return weights * lax.rsqrt(power - window * window / tap_count + tap_count * 1e-06)


def keep_rolled(ext, rolled_ref):
    chan_count, length = ext.shape
    for i in range(ROWS):
        shifted = rolled_left(ext, i)
        for b in range(length // LANES):
            rolled_ref[b, i * chan_count:(i + 1) * chan_count, :] = shifted[:, b * LANES:(b + 1) * LANES]


def lag_matrix(rolled_ref, channel, chan_count, tap_count, lag_count):
    blocks = [rolled_ref[b, pl.ds(channel, ROWS, stride=chan_count), :] for b in range(rolled_ref.shape[0])]
    base = jnp.concatenate(blocks, axis=1).astype(jnp.bfloat16)
    pieces = [rolled_left(base, g * ROWS)[:, :lag_count] for g in range(tap_count // ROWS)]
    return jnp.concatenate(pieces, axis=0)


def aligned_sum(place, lagged_of, blocks, chan_count):
    lane = lax.broadcasted_iota(jnp.int32, (8, LANES), 1)
    totals = [jnp.zeros((8, LANES), jnp.float32)] * blocks
    for c in range(chan_count):
        shift = place(c)
        source = (lane + shift) & (LANES - 1)
        stays = lane >= shift
        for b in range(blocks):
            mixed = jnp.where(stays, lagged_of(c, b), lagged_of(c, b + 1))
            totals[b] = totals[b] + jnp.take_along_axis(mixed, source, axis=1, mode="promise_in_bounds")
    return jnp.concatenate(totals, axis=1)


def band_scale(ext, weights, band, tap_count):
    f32 = jnp.float32
    chan_count = ext.shape[0]
    squares = ext * ext
    high = squares.astype(jnp.bfloat16).astype(f32)
    stacked = jnp.concatenate([ext, high, squares - high, jnp.zeros_like(ext)], axis=0).astype(jnp.bfloat16)
    totals = jnp.dot(stacked, band, preferred_element_type=f32)
    window = totals[:chan_count]
    power = totals[chan_count:2 * chan_count] + totals[2 * chan_count:3 * chan_count]
    return weights * lax.rsqrt(power - window * window / tap_count + tap_count * 1e-06)


def early_kernel(rec_hbm, tail_hbm, templ_hbm, shift_hbm, mask_hbm,
                 unit_out, shift_out, border_out, first_out, edge_out, weight_out, band_out,
                 rec_ref, tail_ref, templ_ref, shift_ref, mask_ref, unit_ref, rolled_ref, prod_ref, sems):
    f32 = jnp.float32
    chan_count = rec_ref.shape[0]
    templ_count = first_out.shape[0]
    tap_count = templ_ref.shape[1]
    lag_count = prod_ref.shape[2]
    blocks = first_out.shape[1] // LANES
    copies = [pltpu.make_async_copy(src, dst, sems.at[n]) for n, (src, dst) in enumerate(
        ((templ_hbm, templ_ref), (rec_hbm, rec_ref), (shift_hbm, shift_ref), (mask_hbm, mask_ref), (tail_hbm, tail_ref)))]
    for copy in copies:
        copy.start()
    for copy in copies:
        copy.wait()

    values = templ_ref[...].astype(f32)
    ones = jnp.ones((tap_count, LANES), jnp.bfloat16)
    centered = values - jnp.dot(templ_ref[...], ones, preferred_element_type=f32) / tap_count
    squares = centered * centered
    high = squares.astype(jnp.bfloat16)
    low = (squares - high.astype(f32)).astype(jnp.bfloat16)
    power = (jnp.dot(high, ones, preferred_element_type=f32) + jnp.dot(low, ones, preferred_element_type=f32)) / tap_count
    unit_ref[...] = centered * lax.rsqrt(tap_count * (power + 1e-06))

    ext = rec_ref[...].astype(f32)
    weights = jnp.transpose(mask_ref[...]).astype(f32)
    shape = (ext.shape[1], lag_count)
    span = lax.broadcasted_iota(jnp.int32, shape, 0) - lax.broadcasted_iota(jnp.int32, shape, 1)
    band_all = jnp.where((span >= 0) & (span < tap_count), 1.0, 0.0).astype(jnp.bfloat16)
    band_out[...] = band_all[:band_out.shape[0], :band_out.shape[1]]
    weight_out[...] = jnp.broadcast_to(weights, (chan_count, LANES))
    halo_len = tail_ref.shape[1]
    edge_out[...] = jnp.zeros(edge_out.shape, f32)
    edge_out[:, :LANES] = ext[:, ext.shape[1] - LANES:]
    edge_out[:, LANES:LANES + halo_len] = tail_ref[...].astype(f32)
    scale = band_scale(ext, weights, band_all, tap_count)
    keep_rolled(ext, rolled_ref)
    shifts = jnp.transpose(shift_ref[...]).astype(f32).astype(jnp.bfloat16)
    pick = lax.broadcasted_iota(jnp.int32, (chan_count, chan_count * LANES), 1) // LANES
    pick = (pick == lax.broadcasted_iota(jnp.int32, pick.shape, 0)).astype(f32).astype(jnp.bfloat16)
    spread_shifts = jnp.dot(shifts, pick, preferred_element_type=f32).astype(jnp.int32)
    for c in range(chan_count):
        lagged = lag_matrix(rolled_ref, c, chan_count, tap_count, lag_count)
        unit = unit_ref[pl.ds(c, templ_count, stride=chan_count), :].astype(jnp.bfloat16)
        unit_out[c] = unit
        product = jnp.dot(unit, lagged, preferred_element_type=f32) * scale[c:c + 1, :lag_count]
        prod_ref[c] = product
        border_out[c] = product[:, lag_count - LANES:]
        shift_out[c] = spread_shifts[:, c * LANES:(c + 1) * LANES]
    for k in range(0, templ_count, ROWS):
        halves = [aligned_sum(lambda c: shift_out[c, r:r + 8, :],
                              lambda c, b: prod_ref[c, r:r + 8, b * LANES:(b + 1) * LANES],
                              blocks, chan_count) for r in (k, k + 8)]
        first_out[k:k + ROWS, :] = jnp.concatenate(halves, axis=0).astype(jnp.bfloat16)


def late_kernel(axis, even_ref, odd_ref, edge_ref, weight_ref, unit_ref, shift_ref, border_ref, first_ref, band_ref, out_ref,
                ext_ref, rolled_ref, prod_ref):
    f32 = jnp.float32
    chan_count = even_ref.shape[0]
    templ_count, first_len = first_ref.shape
    tap_count = unit_ref.shape[2]
    lag_count = prod_ref.shape[2]
    blocks = lag_count // LANES
    out_len = first_len + lag_count
    place = lax.axis_index(axis)
    at_end = place == lax.axis_size(axis) - 1
    is_odd = lax.rem(place, 2) == 1
    ext_ref[...] = edge_ref[...]

    @pl.when(jnp.logical_not(is_odd))
    def _():
        ext_ref[:, LANES:] = even_ref[:, :2 * LANES].astype(f32)

    @pl.when(jnp.logical_and(is_odd, jnp.logical_not(at_end)))
    def _():
        ext_ref[:, LANES:] = odd_ref[:, :2 * LANES].astype(f32)

    ext = ext_ref[...]
    weights = weight_ref[...]
    keep_rolled(ext, rolled_ref)
    scale = band_scale(ext, weights[:, :1], band_ref[...], tap_count)
    for c in range(chan_count):
        lagged = lag_matrix(rolled_ref, c, chan_count, tap_count, lag_count)
        prod_ref[c] = jnp.dot(unit_ref[c], lagged, preferred_element_type=f32) * scale[c:c + 1, :lag_count]
    for k in range(0, templ_count, ROWS):
        def lagged_of(c, b):
            rows = slice(r, r + 8)
            return border_ref[c, rows, :] if b == 0 else prod_ref[c, rows, (b - 1) * LANES:b * LANES]
        halves = []
        for r in (k, k + 8):
            halves.append(aligned_sum(lambda c: shift_ref[c, r:r + 8, :], lagged_of, blocks, chan_count))
        out_ref[k:k + ROWS, first_len:out_len] = jnp.concatenate(halves, axis=0).astype(jnp.bfloat16)
    out_ref[:, :first_len] = first_ref[...]
    count = jnp.sum(weights, axis=0, keepdims=True)
    out_ref[:, out_len:] = jnp.broadcast_to(count, (templ_count, LANES)).astype(jnp.bfloat16)


def shards(record, tail, templates, shifts, mask):
    templ_count, chan_count, tap_count = templates.shape
    out_len = record.shape[1]
    early_len = out_len - LANES
    first_len = early_len - LANES
    f32, bf16 = jnp.float32, jnp.bfloat16
    vmem = pl.BlockSpec(memory_space=pltpu.VMEM)
    hbm = pl.BlockSpec(memory_space=pltpu.HBM)
    params = pltpu.CompilerParams(vmem_limit_bytes=VMEM_BYTES)
    size = lax.axis_size("tm")
    mask_row = mask.reshape(1, chan_count)
    even_odd = [(i, i ^ 1) for i in range(size)]
    ends = (0, size - 1)
    odd_even = []
    for group in range(lax.axis_size("chan")):
        for i in range(size):
            to = (group ^ 1, i) if i in ends else (group, ((i - 1) ^ 1) + 1)
            odd_even.append((group * size + i, to[0] * size + to[1]))
    to_even = lax.ppermute(record, "tm", even_odd)
    to_odd = lax.ppermute(record, ("chan", "tm"), odd_even)
    unit, moved, border, first, edge, weights, band = pl.pallas_call(
        early_kernel,
        out_shape=(
            jax.ShapeDtypeStruct((chan_count, templ_count, tap_count), bf16),
            jax.ShapeDtypeStruct((chan_count, templ_count, LANES), jnp.int32),
            jax.ShapeDtypeStruct((chan_count, templ_count, LANES), f32),
            jax.ShapeDtypeStruct((templ_count, first_len), bf16),
            jax.ShapeDtypeStruct((chan_count, 3 * LANES), f32),
            jax.ShapeDtypeStruct((chan_count, LANES), f32),
            jax.ShapeDtypeStruct((3 * LANES, 2 * LANES), bf16),
        ),
        in_specs=[hbm] * 5,
        out_specs=(vmem,) * 7,
        scratch_shapes=[
            pltpu.VMEM((chan_count, out_len), bf16),
            pltpu.VMEM(tail.shape, bf16),
            pltpu.VMEM((templ_count * chan_count, tap_count), bf16),
            pltpu.VMEM((chan_count, templ_count), jnp.int32),
            pltpu.VMEM((1, chan_count), jnp.int32),
            pltpu.VMEM((templ_count * chan_count, tap_count), f32),
            pltpu.VMEM((out_len // LANES, ROWS * chan_count, LANES), f32),
            pltpu.VMEM((chan_count, templ_count, early_len), f32),
            pltpu.SemaphoreType.DMA((5,)),
        ],
        compiler_params=params,
        cost_estimate=pl.CostEstimate(flops=200_000_000, bytes_accessed=2_000_000, transcendentals=0),
        name="early_lags",
    )(*[pltpu.with_memory_space_constraint(x, pltpu.HBM) for x in (
        record, tail, templates.reshape(templ_count * chan_count, tap_count), shifts.T, mask_row)])
    partial = pl.pallas_call(
        lambda *refs: late_kernel("tm", *refs),
        out_shape=jax.ShapeDtypeStruct((templ_count, out_len + LANES), bf16),
        in_specs=[vmem] * 9,
        out_specs=vmem,
        scratch_shapes=[
            pltpu.VMEM((chan_count, 3 * LANES), f32),
            pltpu.VMEM((3, ROWS * chan_count, LANES), f32),
            pltpu.VMEM((chan_count, templ_count, 2 * LANES), f32),
        ],
        compiler_params=params,
        name="late_lags",
    )(to_even, to_odd, edge, weights, unit, moved, border, first, band)
    tiles = partial.reshape(lax.axis_size("chan"), -1, partial.shape[1])
    arrived = lax.all_to_all(tiles, "chan", split_axis=0, concat_axis=0, tiled=True)
    summed = jnp.sum(arrived.astype(f32), axis=0)
    count = jnp.maximum(summed[:, out_len:out_len + 1], 1.0)
    return summed[:, :out_len] * jnp.sqrt(tap_count / count)


def solution(mesh):
    in_specs = (P("chan", "tm"), P("chan", None), P(None, "chan", None), P(None, "chan"), P("chan"))
    return jax.shard_map(shards, mesh=mesh, in_specs=in_specs, out_specs=P("chan", "tm"), check_vma=False)
```

```python
import jax
import jax.numpy as jnp
from jax import lax
from jax.experimental import pallas as pl
from jax.experimental.pallas import tpu as pltpu
from jax.sharding import PartitionSpec as P

LANES = 128
ROWS = 16
VMEM_BYTES = 32 * 1024 * 1024


def rolled_left(x, distance):
    if distance == 0:
        return x
    return pltpu.roll(x, x.shape[1] - distance, 1)


def window_total(x, tap_count):
    width = 1
    while width < tap_count:
        x = x + rolled_left(x, width)
        width *= 2
    return x


def window_scale(ext, weights, tap_count):
    window = window_total(ext, tap_count)
    power = window_total(ext * ext, tap_count)
    return weights * lax.rsqrt(power - window * window / tap_count + tap_count * 1e-06)


def keep_rolled(ext, rolled_ref):
    chan_count, length = ext.shape
    for i in range(ROWS):
        shifted = rolled_left(ext, i)
        for b in range(length // LANES):
            rolled_ref[b, i * chan_count:(i + 1) * chan_count, :] = shifted[:, b * LANES:(b + 1) * LANES]


def lag_matrix(rolled_ref, channel, chan_count, tap_count, lag_count):
    blocks = [rolled_ref[b, pl.ds(channel, ROWS, stride=chan_count), :] for b in range(rolled_ref.shape[0])]
    base = jnp.concatenate(blocks, axis=1).astype(jnp.bfloat16)
    pieces = [rolled_left(base, g * ROWS)[:, :lag_count] for g in range(tap_count // ROWS)]
    return jnp.concatenate(pieces, axis=0)


def aligned_sum(place, lagged_of, blocks, chan_count):
    lane = lax.broadcasted_iota(jnp.int32, (8, LANES), 1)
    totals = [jnp.zeros((8, LANES), jnp.float32)] * blocks
    for c in range(chan_count):
        shift = place(c)
        source = (lane + shift) & (LANES - 1)
        stays = lane >= shift
        for b in range(blocks):
            mixed = jnp.where(stays, lagged_of(c, b), lagged_of(c, b + 1))
            totals[b] = totals[b] + jnp.take_along_axis(mixed, source, axis=1, mode="promise_in_bounds")
    return jnp.concatenate(totals, axis=1)


def band_scale(ext, weights, band, tap_count):
    f32 = jnp.float32
    chan_count = ext.shape[0]
    squares = ext * ext
    high = squares.astype(jnp.bfloat16).astype(f32)
    stacked = jnp.concatenate([ext, high, squares - high, jnp.zeros_like(ext)], axis=0).astype(jnp.bfloat16)
    totals = jnp.dot(stacked, band, preferred_element_type=f32)
    window = totals[:chan_count]
    power = totals[chan_count:2 * chan_count] + totals[2 * chan_count:3 * chan_count]
    return weights * lax.rsqrt(power - window * window / tap_count + tap_count * 1e-06)


def early_kernel(rec_hbm, tail_hbm, templ_hbm, shift_hbm, mask_hbm,
                 unit_out, shift_out, border_out, first_out, edge_out, weight_out, band_out,
                 rec_ref, tail_ref, templ_ref, shift_ref, mask_ref, unit_ref, rolled_ref, prod_ref, sems):
    f32 = jnp.float32
    chan_count = rec_ref.shape[0]
    templ_count = first_out.shape[0]
    tap_count = templ_ref.shape[1]
    lag_count = prod_ref.shape[2]
    blocks = first_out.shape[1] // LANES
    copies = [pltpu.make_async_copy(src, dst, sems.at[n]) for n, (src, dst) in enumerate(
        ((templ_hbm, templ_ref), (rec_hbm, rec_ref), (shift_hbm, shift_ref), (mask_hbm, mask_ref), (tail_hbm, tail_ref)))]
    for copy in copies:
        copy.start()
    for copy in copies:
        copy.wait()

    values = templ_ref[...].astype(f32)
    ones = jnp.ones((tap_count, LANES), jnp.bfloat16)
    centered = values - jnp.dot(templ_ref[...], ones, preferred_element_type=f32) / tap_count
    squares = centered * centered
    high = squares.astype(jnp.bfloat16)
    low = (squares - high.astype(f32)).astype(jnp.bfloat16)
    power = (jnp.dot(high, ones, preferred_element_type=f32) + jnp.dot(low, ones, preferred_element_type=f32)) / tap_count
    unit_ref[...] = centered * lax.rsqrt(tap_count * (power + 1e-06))

    ext = rec_ref[...].astype(f32)
    weights = jnp.transpose(mask_ref[...]).astype(f32)
    shape = (ext.shape[1], lag_count)
    span = lax.broadcasted_iota(jnp.int32, shape, 0) - lax.broadcasted_iota(jnp.int32, shape, 1)
    band_all = jnp.where((span >= 0) & (span < tap_count), 1.0, 0.0).astype(jnp.bfloat16)
    band_out[...] = band_all[:band_out.shape[0], :band_out.shape[1]]
    weight_out[...] = jnp.broadcast_to(weights, (chan_count, LANES))
    halo_len = tail_ref.shape[1]
    edge_out[...] = jnp.zeros(edge_out.shape, f32)
    edge_out[:, :LANES] = ext[:, ext.shape[1] - LANES:]
    edge_out[:, LANES:LANES + halo_len] = tail_ref[...].astype(f32)
    scale = band_scale(ext, weights, band_all, tap_count)
    keep_rolled(ext, rolled_ref)
    shifts = jnp.transpose(shift_ref[...]).astype(f32).astype(jnp.bfloat16)
    pick = lax.broadcasted_iota(jnp.int32, (chan_count, chan_count * LANES), 1) // LANES
    pick = (pick == lax.broadcasted_iota(jnp.int32, pick.shape, 0)).astype(f32).astype(jnp.bfloat16)
    spread_shifts = jnp.dot(shifts, pick, preferred_element_type=f32).astype(jnp.int32)
    for c in range(chan_count):
        lagged = lag_matrix(rolled_ref, c, chan_count, tap_count, lag_count)
        unit = unit_ref[pl.ds(c, templ_count, stride=chan_count), :].astype(jnp.bfloat16)
        unit_out[c] = unit
        product = jnp.dot(unit, lagged, preferred_element_type=f32) * scale[c:c + 1, :lag_count]
        prod_ref[c] = product
        border_out[c] = product[:, lag_count - LANES:]
        shift_out[c] = spread_shifts[:, c * LANES:(c + 1) * LANES]
    for k in range(0, templ_count, ROWS):
        halves = [aligned_sum(lambda c: shift_out[c, r:r + 8, :],
                              lambda c, b: prod_ref[c, r:r + 8, b * LANES:(b + 1) * LANES],
                              blocks, chan_count) for r in (k, k + 8)]
        first_out[k:k + ROWS, :] = jnp.concatenate(halves, axis=0).astype(jnp.bfloat16)


def aligned_half(place, lagged_of, blocks, chan_count):
    lane = lax.broadcasted_iota(jnp.int32, (ROWS, LANES), 1)
    totals = [jnp.zeros((ROWS, LANES), jnp.float32)] * blocks
    for c in range(chan_count):
        shift = place(c)
        source = ((lane + shift) & (LANES - 1)).astype(jnp.int16)
        stays = lane >= shift
        for b in range(blocks):
            mixed = jnp.where(stays, lagged_of(c, b), lagged_of(c, b + 1)).astype(jnp.bfloat16)
            moved = lax.gather(
                mixed, source[:, :, None],
                lax.GatherDimensionNumbers(
                    offset_dims=(), collapsed_slice_dims=(1,), start_index_map=(1,),
                    operand_batching_dims=(0,), start_indices_batching_dims=(0,)),
                (1, 1), mode=lax.GatherScatterMode.PROMISE_IN_BOUNDS)
            totals[b] = totals[b] + moved.astype(jnp.float32)
    return jnp.concatenate(totals, axis=1)


def late_kernel(axis, even_ref, odd_ref, edge_ref, weight_ref, unit_ref, shift_ref, border_ref, first_ref, band_ref, out_ref,
                ext_ref, rolled_ref, prod_ref):
    f32 = jnp.float32
    chan_count = even_ref.shape[0]
    templ_count, first_len = first_ref.shape
    tap_count = unit_ref.shape[2]
    lag_count = prod_ref.shape[2]
    blocks = lag_count // LANES
    out_len = first_len + lag_count
    place = lax.axis_index(axis)
    at_end = place == lax.axis_size(axis) - 1
    is_odd = lax.rem(place, 2) == 1
    ext_ref[...] = edge_ref[...]

    @pl.when(jnp.logical_not(is_odd))
    def _():
        ext_ref[:, LANES:] = even_ref[:, :2 * LANES].astype(f32)

    @pl.when(jnp.logical_and(is_odd, jnp.logical_not(at_end)))
    def _():
        ext_ref[:, LANES:] = odd_ref[:, :2 * LANES].astype(f32)

    ext = ext_ref[...]
    weights = weight_ref[...]
    keep_rolled(ext, rolled_ref)
    scale = band_scale(ext, weights[:, :1], band_ref[...], tap_count)
    for c in range(chan_count):
        lagged = lag_matrix(rolled_ref, c, chan_count, tap_count, lag_count)
        prod_ref[c] = jnp.dot(unit_ref[c], lagged, preferred_element_type=f32) * scale[c:c + 1, :lag_count]
    for k in range(0, templ_count, ROWS):
        def lagged_of(c, b):
            rows = slice(r, r + ROWS)
            return border_ref[c, rows, :] if b == 0 else prod_ref[c, rows, (b - 1) * LANES:b * LANES]
        r = k
        both = aligned_half(lambda c: shift_ref[c, k:k + ROWS, :], lagged_of, blocks, chan_count)
        out_ref[k:k + ROWS, first_len:out_len] = both.astype(jnp.bfloat16)
    out_ref[:, :first_len] = first_ref[...]
    count = jnp.sum(weights, axis=0, keepdims=True)
    out_ref[:, out_len:] = jnp.broadcast_to(count, (templ_count, LANES)).astype(jnp.bfloat16)


def shards(record, tail, templates, shifts, mask):
    templ_count, chan_count, tap_count = templates.shape
    out_len = record.shape[1]
    early_len = out_len - LANES
    first_len = early_len - LANES
    f32, bf16 = jnp.float32, jnp.bfloat16
    vmem = pl.BlockSpec(memory_space=pltpu.VMEM)
    hbm = pl.BlockSpec(memory_space=pltpu.HBM)
    params = pltpu.CompilerParams(vmem_limit_bytes=VMEM_BYTES)
    size = lax.axis_size("tm")
    mask_row = mask.reshape(1, chan_count)
    even_odd = [(i, i ^ 1) for i in range(size)]
    ends = (0, size - 1)
    odd_even = []
    for group in range(lax.axis_size("chan")):
        for i in range(size):
            to = (group ^ 1, i) if i in ends else (group, ((i - 1) ^ 1) + 1)
            odd_even.append((group * size + i, to[0] * size + to[1]))
    to_even = lax.ppermute(record, "tm", even_odd)
    to_odd = lax.ppermute(record, ("chan", "tm"), odd_even)
    unit, moved, border, first, edge, weights, band = pl.pallas_call(
        early_kernel,
        out_shape=(
            jax.ShapeDtypeStruct((chan_count, templ_count, tap_count), bf16),
            jax.ShapeDtypeStruct((chan_count, templ_count, LANES), jnp.int32),
            jax.ShapeDtypeStruct((chan_count, templ_count, LANES), f32),
            jax.ShapeDtypeStruct((templ_count, first_len), bf16),
            jax.ShapeDtypeStruct((chan_count, 3 * LANES), f32),
            jax.ShapeDtypeStruct((chan_count, LANES), f32),
            jax.ShapeDtypeStruct((3 * LANES, 2 * LANES), bf16),
        ),
        in_specs=[hbm] * 5,
        out_specs=(vmem,) * 7,
        scratch_shapes=[
            pltpu.VMEM((chan_count, out_len), bf16),
            pltpu.VMEM(tail.shape, bf16),
            pltpu.VMEM((templ_count * chan_count, tap_count), bf16),
            pltpu.VMEM((chan_count, templ_count), jnp.int32),
            pltpu.VMEM((1, chan_count), jnp.int32),
            pltpu.VMEM((templ_count * chan_count, tap_count), f32),
            pltpu.VMEM((out_len // LANES, ROWS * chan_count, LANES), f32),
            pltpu.VMEM((chan_count, templ_count, early_len), f32),
            pltpu.SemaphoreType.DMA((5,)),
        ],
        compiler_params=params,
        cost_estimate=pl.CostEstimate(flops=200_000_000, bytes_accessed=2_000_000, transcendentals=0),
        name="early_lags",
    )(*[pltpu.with_memory_space_constraint(x, pltpu.HBM) for x in (
        record, tail, templates.reshape(templ_count * chan_count, tap_count), shifts.T, mask_row)])
    partial = pl.pallas_call(
        lambda *refs: late_kernel("tm", *refs),
        out_shape=jax.ShapeDtypeStruct((templ_count, out_len + LANES), bf16),
        in_specs=[vmem] * 9,
        out_specs=vmem,
        scratch_shapes=[
            pltpu.VMEM((chan_count, 3 * LANES), f32),
            pltpu.VMEM((3, ROWS * chan_count, LANES), f32),
            pltpu.VMEM((chan_count, templ_count, 2 * LANES), f32),
        ],
        compiler_params=params,
        name="late_lags",
    )(to_even, to_odd, edge, weights, unit, moved, border, first, band)
    tiles = partial.reshape(lax.axis_size("chan"), -1, partial.shape[1])
    arrived = lax.all_to_all(tiles, "chan", split_axis=0, concat_axis=0, tiled=True)
    summed = jnp.sum(arrived.astype(f32), axis=0)
    count = jnp.maximum(summed[:, out_len:out_len + 1], 1.0)
    return summed[:, :out_len] * jnp.sqrt(tap_count / count)


def solution(mesh):
    in_specs = (P("chan", "tm"), P("chan", None), P(None, "chan", None), P(None, "chan"), P("chan"))
    return jax.shard_map(shards, mesh=mesh, in_specs=in_specs, out_specs=P("chan", "tm"), check_vma=False)
```

```python
import jax
import jax.numpy as jnp
from jax import lax
from jax.experimental import pallas as pl
from jax.experimental.pallas import tpu as pltpu
from jax.sharding import PartitionSpec as P

LANES = 128
ROWS = 16
VMEM_BYTES = 32 * 1024 * 1024


def rolled_left(x, distance):
    if distance == 0:
        return x
    return pltpu.roll(x, x.shape[1] - distance, 1)


def window_total(x, tap_count):
    width = 1
    while width < tap_count:
        x = x + rolled_left(x, width)
        width *= 2
    return x


def window_scale(ext, weights, tap_count):
    window = window_total(ext, tap_count)
    power = window_total(ext * ext, tap_count)
    return weights * lax.rsqrt(power - window * window / tap_count + tap_count * 1e-06)


def keep_rolled(ext, rolled_ref):
    chan_count, length = ext.shape
    for i in range(ROWS):
        shifted = rolled_left(ext, i)
        for b in range(length // LANES):
            rolled_ref[b, i * chan_count:(i + 1) * chan_count, :] = shifted[:, b * LANES:(b + 1) * LANES]


def lag_matrix(rolled_ref, channel, chan_count, tap_count, lag_count):
    blocks = [rolled_ref[b, pl.ds(channel, ROWS, stride=chan_count), :] for b in range(rolled_ref.shape[0])]
    base = jnp.concatenate(blocks, axis=1).astype(jnp.bfloat16)
    pieces = [rolled_left(base, g * ROWS)[:, :lag_count] for g in range(tap_count // ROWS)]
    return jnp.concatenate(pieces, axis=0)


def aligned_sum(place, lagged_of, blocks, chan_count):
    lane = lax.broadcasted_iota(jnp.int32, (8, LANES), 1)
    totals = [jnp.zeros((8, LANES), jnp.float32)] * blocks
    for c in range(chan_count):
        shift = place(c)
        source = (lane + shift) & (LANES - 1)
        stays = lane >= shift
        for b in range(blocks):
            mixed = jnp.where(stays, lagged_of(c, b), lagged_of(c, b + 1))
            totals[b] = totals[b] + jnp.take_along_axis(mixed, source, axis=1, mode="promise_in_bounds")
    return jnp.concatenate(totals, axis=1)


def band_scale(ext, weights, band, tap_count):
    f32 = jnp.float32
    chan_count = ext.shape[0]
    squares = ext * ext
    high = squares.astype(jnp.bfloat16).astype(f32)
    stacked = jnp.concatenate([ext, high, squares - high, jnp.zeros_like(ext)], axis=0).astype(jnp.bfloat16)
    totals = jnp.dot(stacked, band, preferred_element_type=f32)
    window = totals[:chan_count]
    power = totals[chan_count:2 * chan_count] + totals[2 * chan_count:3 * chan_count]
    return weights * lax.rsqrt(power - window * window / tap_count + tap_count * 1e-06)


def early_kernel(rec_hbm, tail_hbm, templ_hbm, shift_hbm, mask_hbm,
                 unit_out, shift_out, border_out, first_out, edge_out, weight_out, band_out,
                 rec_ref, tail_ref, templ_ref, shift_ref, mask_ref, unit_ref, rolled_ref, prod_ref, sems):
    f32 = jnp.float32
    chan_count = rec_ref.shape[0]
    templ_count = first_out.shape[0]
    tap_count = templ_ref.shape[1]
    lag_count = prod_ref.shape[2]
    blocks = first_out.shape[1] // LANES
    copies = [pltpu.make_async_copy(src, dst, sems.at[n]) for n, (src, dst) in enumerate(
        ((templ_hbm, templ_ref), (rec_hbm, rec_ref), (shift_hbm, shift_ref), (mask_hbm, mask_ref), (tail_hbm, tail_ref)))]
    for copy in copies:
        copy.start()
    for copy in copies:
        copy.wait()

    values = templ_ref[...].astype(f32)
    ones = jnp.ones((tap_count, LANES), jnp.bfloat16)
    centered = values - jnp.dot(templ_ref[...], ones, preferred_element_type=f32) / tap_count
    squares = centered * centered
    high = squares.astype(jnp.bfloat16)
    low = (squares - high.astype(f32)).astype(jnp.bfloat16)
    power = (jnp.dot(high, ones, preferred_element_type=f32) + jnp.dot(low, ones, preferred_element_type=f32)) / tap_count
    unit_ref[...] = centered * lax.rsqrt(tap_count * (power + 1e-06))

    ext = rec_ref[...].astype(f32)
    weights = jnp.transpose(mask_ref[...]).astype(f32)
    shape = (ext.shape[1], lag_count)
    span = lax.broadcasted_iota(jnp.int32, shape, 0) - lax.broadcasted_iota(jnp.int32, shape, 1)
    band_all = jnp.where((span >= 0) & (span < tap_count), 1.0, 0.0).astype(jnp.bfloat16)
    band_out[...] = band_all[:band_out.shape[0], :band_out.shape[1]]
    weight_out[...] = jnp.broadcast_to(weights, (chan_count, LANES))
    halo_len = tail_ref.shape[1]
    edge_out[...] = jnp.zeros(edge_out.shape, f32)
    edge_out[:, :LANES] = ext[:, ext.shape[1] - LANES:]
    edge_out[:, LANES:LANES + halo_len] = tail_ref[...].astype(f32)
    scale = band_scale(ext, weights, band_all, tap_count)
    keep_rolled(ext, rolled_ref)
    shifts = jnp.transpose(shift_ref[...]).astype(f32).astype(jnp.bfloat16)
    pick = lax.broadcasted_iota(jnp.int32, (chan_count, chan_count * LANES), 1) // LANES
    pick = (pick == lax.broadcasted_iota(jnp.int32, pick.shape, 0)).astype(f32).astype(jnp.bfloat16)
    spread_shifts = jnp.dot(shifts, pick, preferred_element_type=f32).astype(jnp.int32)
    for c in range(chan_count):
        lagged = lag_matrix(rolled_ref, c, chan_count, tap_count, lag_count)
        unit = unit_ref[pl.ds(c, templ_count, stride=chan_count), :].astype(jnp.bfloat16)
        unit_out[c] = unit
        product = jnp.dot(unit, lagged, preferred_element_type=f32) * scale[c:c + 1, :lag_count]
        prod_ref[c] = product
        border_out[c] = product[:, lag_count - LANES:]
        shift_out[c] = spread_shifts[:, c * LANES:(c + 1) * LANES]
    for k in range(0, templ_count, ROWS):
        halves = [aligned_sum(lambda c: shift_out[c, r:r + 8, :],
                              lambda c, b: prod_ref[c, r:r + 8, b * LANES:(b + 1) * LANES],
                              blocks, chan_count) for r in (k, k + 8)]
        first_out[k:k + ROWS, :] = jnp.concatenate(halves, axis=0).astype(jnp.bfloat16)


def aligned_half(place, lagged_of, blocks, chan_count):
    lane = lax.broadcasted_iota(jnp.int32, (ROWS, LANES), 1)
    totals = [jnp.zeros((ROWS, LANES), jnp.float32)] * blocks
    for c in range(chan_count):
        shift = place(c)
        source = ((lane + shift) & (LANES - 1)).astype(jnp.int16)
        stays = lane >= shift
        for b in range(blocks):
            mixed = jnp.where(stays, lagged_of(c, b), lagged_of(c, b + 1)).astype(jnp.bfloat16)
            moved = lax.gather(
                mixed, source[:, :, None],
                lax.GatherDimensionNumbers(
                    offset_dims=(), collapsed_slice_dims=(1,), start_index_map=(1,),
                    operand_batching_dims=(0,), start_indices_batching_dims=(0,)),
                (1, 1), mode=lax.GatherScatterMode.PROMISE_IN_BOUNDS)
            totals[b] = totals[b] + moved.astype(jnp.float32)
    return jnp.concatenate(totals, axis=1)


def late_kernel(axis, even_ref, odd_ref, edge_ref, weight_ref, unit_ref, shift_ref, border_ref, first_ref, band_ref, out_ref,
                ext_ref, rolled_ref, prod_ref):
    f32 = jnp.float32
    chan_count = even_ref.shape[0]
    templ_count, first_len = first_ref.shape
    tap_count = unit_ref.shape[2]
    lag_count = prod_ref.shape[2]
    blocks = lag_count // LANES
    out_len = first_len + lag_count
    place = lax.axis_index(axis)
    at_end = place == lax.axis_size(axis) - 1
    is_odd = lax.rem(place, 2) == 1
    ext_ref[...] = edge_ref[...]

    @pl.when(jnp.logical_not(is_odd))
    def _():
        ext_ref[:, LANES:] = even_ref[:, :2 * LANES].astype(f32)

    @pl.when(jnp.logical_and(is_odd, jnp.logical_not(at_end)))
    def _():
        ext_ref[:, LANES:] = odd_ref[:, :2 * LANES].astype(f32)

    ext = ext_ref[...]
    weights = weight_ref[...]
    keep_rolled(ext, rolled_ref)
    scale = band_scale(ext, weights[:, :1], band_ref[...], tap_count)
    for c in range(chan_count):
        lagged = lag_matrix(rolled_ref, c, chan_count, tap_count, lag_count)
        prod_ref[c] = jnp.dot(unit_ref[c], lagged, preferred_element_type=f32) * scale[c:c + 1, :lag_count]
    for k in range(0, templ_count, ROWS):
        def lagged_of(c, b):
            rows = slice(r, r + ROWS)
            return border_ref[c, rows, :] if b == 0 else prod_ref[c, rows, (b - 1) * LANES:b * LANES]
        r = k
        both = aligned_half(lambda c: shift_ref[c, k:k + ROWS, :], lagged_of, blocks, chan_count)
        out_ref[k:k + ROWS, first_len:out_len] = both.astype(jnp.bfloat16)
    out_ref[:, :first_len] = first_ref[...]
    count = jnp.sum(weights, axis=0, keepdims=True)
    out_ref[:, out_len:] = jnp.broadcast_to(count, (templ_count, LANES)).astype(jnp.bfloat16)


def shards(record, tail, templates, shifts, mask):
    templ_count, chan_count, tap_count = templates.shape
    out_len = record.shape[1]
    early_len = out_len - LANES
    first_len = early_len - LANES
    f32, bf16 = jnp.float32, jnp.bfloat16
    vmem = pl.BlockSpec(memory_space=pltpu.VMEM)
    hbm = pl.BlockSpec(memory_space=pltpu.HBM)
    params = pltpu.CompilerParams(vmem_limit_bytes=VMEM_BYTES)
    size = lax.axis_size("tm")
    mask_row = mask.reshape(1, chan_count)
    even_odd = [(i, i ^ 1) for i in range(size)]
    ends = (0, size - 1)
    odd_even = []
    for group in range(lax.axis_size("chan")):
        for i in range(size):
            to = (group ^ 1, i) if i in ends else (group, ((i - 1) ^ 1) + 1)
            odd_even.append((group * size + i, to[0] * size + to[1]))
    to_even = lax.ppermute(record, "tm", even_odd)
    to_odd = lax.ppermute(record, ("chan", "tm"), odd_even)
    unit, moved, border, first, edge, weights, band = pl.pallas_call(
        early_kernel,
        out_shape=(
            jax.ShapeDtypeStruct((chan_count, templ_count, tap_count), bf16),
            jax.ShapeDtypeStruct((chan_count, templ_count, LANES), jnp.int32),
            jax.ShapeDtypeStruct((chan_count, templ_count, LANES), f32),
            jax.ShapeDtypeStruct((templ_count, first_len), bf16),
            jax.ShapeDtypeStruct((chan_count, 3 * LANES), f32),
            jax.ShapeDtypeStruct((chan_count, LANES), f32),
            jax.ShapeDtypeStruct((3 * LANES, 2 * LANES), bf16),
        ),
        in_specs=[hbm] * 5,
        out_specs=(vmem,) * 7,
        scratch_shapes=[
            pltpu.VMEM((chan_count, out_len), bf16),
            pltpu.VMEM(tail.shape, bf16),
            pltpu.VMEM((templ_count * chan_count, tap_count), bf16),
            pltpu.VMEM((chan_count, templ_count), jnp.int32),
            pltpu.VMEM((1, chan_count), jnp.int32),
            pltpu.VMEM((templ_count * chan_count, tap_count), f32),
            pltpu.VMEM((out_len // LANES, ROWS * chan_count, LANES), f32),
            pltpu.VMEM((chan_count, templ_count, early_len), f32),
            pltpu.SemaphoreType.DMA((5,)),
        ],
        compiler_params=params,
        cost_estimate=pl.CostEstimate(flops=200_000_000, bytes_accessed=2_000_000, transcendentals=0),
        name="early_lags",
    )(*[pltpu.with_memory_space_constraint(x, pltpu.HBM) for x in (
        record, tail, templates.reshape(templ_count * chan_count, tap_count), shifts.T, mask_row)])
    partial = pl.pallas_call(
        lambda *refs: late_kernel("tm", *refs),
        out_shape=jax.ShapeDtypeStruct((templ_count, out_len + LANES), bf16),
        in_specs=[vmem] * 9,
        out_specs=vmem,
        scratch_shapes=[
            pltpu.VMEM((chan_count, 3 * LANES), f32),
            pltpu.VMEM((3, ROWS * chan_count, LANES), f32),
            pltpu.VMEM((chan_count, templ_count, 2 * LANES), f32),
        ],
        compiler_params=params,
        name="late_lags",
    )(to_even, to_odd, edge, weights, unit, moved, border, first, band)
    tiles = partial.reshape(lax.axis_size("chan"), -1, partial.shape[1])
    arrived = lax.all_to_all(tiles, "chan", split_axis=0, concat_axis=0, tiled=True)
    summed = jnp.sum(arrived.astype(f32), axis=0)
    factor = jnp.sqrt(tap_count / jnp.maximum(summed[:, out_len:], 1.0))
    return jnp.concatenate([summed[:, b:b + LANES] * factor for b in range(0, out_len, LANES)], axis=1)


def solution(mesh):
    in_specs = (P("chan", "tm"), P("chan", None), P(None, "chan", None), P(None, "chan"), P("chan"))
    return jax.shard_map(shards, mesh=mesh, in_specs=in_specs, out_specs=P("chan", "tm"), check_vma=False)
```
